256 devices in a mesh: pw: 64 (over y, x, z_hi, core), tr: 4 (over z_lo).
Axes of the slice: x: 4, y: 4, z: 8 (z_hi: 2, z_lo: 4; z = z_hi * 4 + z_lo), core: 2. Of those that a mesh axis runs over, the one named last changes fastest.
Arguments:
- pair_density: bfloat16 [40960, 4096], P('pw', 'tr'), may hold values from -6 to 6
- basis: bfloat16 [40960, 2048], P('pw'), may hold values from -0.078125 to 0.078125
- block_slot: int32 [4096], P('tr'), may hold values from 0 to 4095, as said below
- energy_code: int32 [4096], P('tr'), may hold values from 32 to 16383
- freq_order: int32 [16], replicated, may hold values from 0 to 15, each once
Outputs:
- chi_sub: float32 [16, 2048, 2048], P('tr', 'pw')
The draws below stay inside these ranges and needn't reach their ends.
Inputs may be any that keep to these rules, and one draw needn't show every extreme that they name: `block_slot`: the 1024 entries of each aligned run starting at a multiple of 1024 are a permutation of that run's own positions.
All inputs are finite; a program needn't handle non-finite values.
Results may differ from the reference program's by a relative error of at most 0.0003.
Values sent between devices are 32-bit elements; how exact they have to be, the bound alone decides.
A program may use at most 64 MiB of HBM per device.

```python
import jax
import jax.numpy as jnp
from jax import lax

NB = 2048
NW = 16
TR_DEV = 1024
NG = 40960
TRANS = 4096


def draw_block_slot(key, part):
    key = jax.random.fold_in(key, 7)
    subkeys = jax.random.split(key, TRANS // TR_DEV)
    orders = jax.vmap(lambda subkey: jax.random.permutation(subkey, TR_DEV))(subkeys)
    offsets = (jnp.arange(TRANS // TR_DEV, dtype=jnp.int32) * TR_DEV)[:, None]
    return (orders.astype(jnp.int32) + offsets).reshape(TRANS)


def place_ends(entries, key, least, high):
    longest = entries.shape.index(max(entries.shape))
    spots = []
    for shift in (0, 1):
        where = [jax.random.randint(jax.random.fold_in(key, axis), (), 0, length) for axis, length in enumerate(entries.shape)]
        where[longest] = (where[longest] + shift) % entries.shape[longest]
        spots.append(tuple(where))
    return entries.at[spots[0]].set(least).at[spots[1]].set(high)


def with_spikes(result, stream_key, source, target, blocks, factor):
    def block_of(position):
        return (jnp.arange(result.shape[position]) // (result.shape[position] // blocks)).reshape((-1,) + (1,) * (result.ndim - 1 - position))

    near = jax.random.permutation(stream_key, blocks)[block_of(target)]
    second = (block_of(target) + blocks // 2) % blocks
    return jnp.where((block_of(source) == near) | (block_of(source) == second), factor * result, result)


def block_scale(key, extent, cuts, smallest, top_value):
    def one(dim, blocks):
        draws = jax.random.uniform(jax.random.fold_in(jax.random.fold_in(key, 6), dim), (blocks,), jnp.float32, smallest / len(cuts), top_value / len(cuts))
        return jnp.repeat(jnp.exp(draws), extent[dim] // blocks).reshape((-1,) + (1,) * (len(extent) - dim - 1))

    factor_of = one(*cuts[0])
    for cut in cuts[1:]:
        factor_of = factor_of * one(*cut)
    return factor_of


def scatter_about(key, shape, scale, limit, pieces=(), kind=jnp.bfloat16):
    level = block_scale(key, shape, pieces, -0.22, 0.18) if pieces else 1.0
    entries = jax.random.normal(key, shape, jnp.float32) * scale * level
    return jnp.minimum(jnp.maximum(entries, -limit), limit).astype(kind)


def noise_with(rng, dims, width, reach, pieces, heavy, kind=jnp.bfloat16):
    values = width * jax.random.normal(rng, dims, jnp.float32)
    if pieces:
        values = values * block_scale(rng, dims, pieces, -0.22, 0.18)
    return jnp.clip(with_spikes(values, jax.random.fold_in(rng, 3), *heavy), -reach, reach).astype(kind)


def setup_inputs(seed: int = 0) -> dict:
    keys = jax.random.split(jax.random.key(seed), 6)
    return {
        "pair_density": scatter_about(keys[0], (NG, TRANS), 1.0, 6.0, ((0, 64), (1, 4))),
        "basis": noise_with(keys[1], (NG, NB), NG ** -0.5, 0.078125, ((0, 64),), (0, 1, 64, 4.0)),
        "block_slot": draw_block_slot(jax.random.fold_in(keys[5], 71), 0),
        "energy_code": place_ends(jax.random.randint(keys[3], (TRANS,), 32, 16384), jax.random.fold_in(keys[3], 1), 32, 16383).astype(jnp.int32),
        "freq_order": jax.random.permutation(keys[4], NW).astype(jnp.int32),
    }


def reference(pair_density, basis, block_slot, energy_code, freq_order):
    energy = energy_code[block_slot].astype(jnp.float32) / 1024.0
    frequency = jnp.exp2(freq_order.astype(jnp.float32) * 0.5 - 4.0)
    weight = 2.0 * energy[None, :] / (energy[None, :] ** 2 + frequency[:, None] ** 2) / TRANS
    projected = lax.dot_general(basis, pair_density, (((0,), (0,)), ((), ())), preferred_element_type=jnp.float32)
    projected_rows = projected.T

    def one_slot(weight_row):
        scaled = projected * weight_row[None, :]
        return jnp.dot(scaled, projected_rows, precision=lax.Precision.HIGHEST, preferred_element_type=jnp.float32)

    return lax.map(one_slot, weight)
```

```python
import functools

import jax
import jax.numpy as jnp
from jax import lax
from jax.experimental import pallas as pl
from jax.experimental.pallas import tpu as pltpu
from jax.sharding import PartitionSpec as P

F32 = jnp.float32
BF16 = jnp.bfloat16
MESH = pl.DeviceIdType.MESH
NC = 4

SLOTS = [
    (0, 0), (0, 1),
    (0, 3), (1, 0),
    (3, 0), (1, 1),
    (1, 3), (3, 1),
    (3, 3), (0, 2),
    (2, 0), (1, 2),
    (3, 2), (2, 1),
    (2, 3), (2, 2),
]
SLOT = {rel: i for i, rel in enumerate(SLOTS)}
NS = len(SLOTS) // 2


def device(y, x, z, core):
    y, x, z = lax.rem(y + 4, 4), lax.rem(x + 4, 4), lax.rem(z + 8, 8)
    return ((y * 4 + x) * 2 + z // 4) * 2 + core, lax.rem(z, 4)


def kernel(
    trans,
    freq_ref, slot_ref, code_ref, pair_hbm, basis_hbm, out_ref,
    pair, basis, basis_t, part, mine, ring1, ring1_sum, ring2, ring2_sum, zrecv,
    proj, energy, weight, gath, lhs_hi, lhs_lo, rhs_hi, rhs_lo, sent, got,
    load_sem, core_s, core_r, ring1_s, ring1_r, ring2_s, ring2_r, z_s, z_r,
    mate_s, mate_r, en_s, en_r, gath_s, gath_r, gcore_s, gcore_r, out_s, out_r,
):
    pw, tr = lax.axis_index("pw"), lax.axis_index("tr")
    core, zh = lax.rem(pw, 2), lax.rem(pw // 2, 2)
    x, y = lax.rem(pw // 4, 4), pw // 16
    z = zh * 4 + tr
    par = lax.rem(z, 2)
    away = 1 - 2 * par

    partner = device(y, x, z, 1 - core)
    ydev = {1: device(y + 1, x, z, core), -1: device(y - 1, x, z, core)}
    xdev = {1: device(y, x + 1, z, core), -1: device(y, x - 1, z, core)}
    opposite = device(y, x, z + 4, core)
    z_mate, z_near, z_far = z + away, z - away, z + 2 * away
    mate, near = device(y, x, z_mate, core), device(y, x, z_near, core)
    far, far_from = device(y, x, z_far, core), device(y, x, z - 2 * away, core)

    load_pair = pltpu.make_async_copy(pair_hbm, pair, load_sem.at[0])
    load_basis = pltpu.make_async_copy(basis_hbm, basis, load_sem.at[1])
    load_basis.start()
    load_pair.start()

    barrier = pltpu.get_barrier_semaphore()
    peers = (partner, ydev[1], ydev[-1], xdev[1], xdev[-1], opposite, mate, near, far, far_from)
    for peer in peers:
        pl.semaphore_signal(barrier, inc=1, device_id=peer, device_id_type=MESH)

    started = []

    def send(src, dst, ssem, rsem, to):
        copy = pltpu.make_async_remote_copy(
            src_ref=src, dst_ref=dst, send_sem=ssem, recv_sem=rsem, device_id=to, device_id_type=MESH
        )
        copy.start()
        started.append(copy)
        return copy

    load_basis.wait()
    basis_t[...] = basis[...].T
    load_pair.wait()
    pl.semaphore_wait(barrier, len(peers))

    place = ((y, x), (x, y))
    line = ((ydev, xdev), (xdev, ydev))
    flight = {}

    def project(c):
        cols = pair[:, 256 * c : 256 * (c + 1)]

        @pl.loop(0, 4)
        def _(i):
            rows = basis_t[pl.ds(pl.multiple_of(i * 512, 512), 512), :]
            block = jnp.dot(rows, cols, preferred_element_type=F32)
            for j in range(4):
                piece = block[128 * j : 128 * (j + 1)]
                part[c, 0, i, j] = piece[:, :128].reshape(2, 2, 32, 128)
                part[c, 1, j, i] = piece[:, 128:].reshape(2, 2, 32, 128)

        flight["core", c] = send(
            part.at[c, :, :, :, :, 1 - core], mine.at[c], core_s.at[c], core_r.at[c], partner
        )

    def ring_open(c, order, stage, block, bufs, ssem, rsem):
        at = place[order][stage]
        up, down = line[order][stage][1], line[order][stage][-1]
        ahead, behind, across = (lax.rem(at + d, 4) for d in (1, 3, 2))
        for i, (src, to) in enumerate(
            ((block(across, 0), up), (block(across, 1), down), (block(ahead, 1), up), (block(behind, 0), down))
        ):
            flight[stage, c, order, i] = send(src, bufs.at[i], ssem.at[i], rsem.at[i], to)

    def ring_pass(c, order, stage, block, bufs, ssem, rsem):
        at = place[order][stage]
        up, down = line[order][stage][1], line[order][stage][-1]
        ahead, behind = lax.rem(at + 1, 4), lax.rem(at + 3, 4)
        for i, (own, to) in enumerate(((block(ahead, 0), up), (block(behind, 1), down))):
            flight[stage, c, order, i].wait_recv()
            bufs[i] = bufs[i] + own[...]
            flight[stage, c, order, 4 + i] = send(
                bufs.at[i], bufs.at[4 + i], ssem.at[4 + i], rsem.at[4 + i], to
            )

    def ring_close(c, order, stage, block, bufs):
        at = place[order][stage]
        for i in (2, 3, 4, 5):
            flight[stage, c, order, i].wait_recv()
        return (
            block(at, 0)[...] + bufs[3] + bufs[4],
            block(at, 1)[...] + bufs[2] + bufs[5],
        )

    def block1(c, order):
        return lambda p, half: mine.at[c, order, p, :, half]

    def block2(c, order):
        return lambda p, half: ring1_sum.at[c, order, p, half]

    def add_core(c):
        flight["core", c].wait_recv()

        @pl.loop(0, 4)
        def _(i):
            mine[c, :, i] = mine[c, :, i] + part[c, :, i, :, :, core]

        for order in (0, 1):
            ring_open(c, order, 0, block1(c, order), ring1.at[c, order], ring1_s.at[c, order], ring1_r.at[c, order])

    def pass1(c):
        for order in (0, 1):
            ring_pass(c, order, 0, block1(c, order), ring1.at[c, order], ring1_s.at[c, order], ring1_r.at[c, order])

    def close1(c):
        for order in (0, 1):
            low, high = ring_close(c, order, 0, block1(c, order), ring1.at[c, order])
            ring1_sum[c, order, :, 0] = low
            ring1_sum[c, order, :, 1] = high
            ring_open(c, order, 1, block2(c, order), ring2.at[c, order], ring2_s.at[c, order], ring2_r.at[c, order])

    def pass2(c):
        for order in (0, 1):
            ring_pass(c, order, 1, block2(c, order), ring2.at[c, order], ring2_s.at[c, order], ring2_r.at[c, order])

    def close2(c):
        for order in (0, 1):
            low, high = ring_close(c, order, 1, block2(c, order), ring2.at[c, order])
            ring2_sum[c, order, 0] = low
            ring2_sum[c, order, 1] = high
        flight["z", c] = send(ring2_sum.at[c], zrecv.at[c], z_s.at[c], z_r.at[c], opposite)

    def close3(c):
        flight["z", c].wait_recv()
        for order in (0, 1):
            first = 256 * c + 128 * order
            proj[0, :, :, first : first + 128] = ring2_sum[c, order] + zrecv[c, order]
        cols = pl.ds(256 * c, 256)
        flight["mate", c] = send(
            proj.at[0, :, :, cols], proj.at[1, :, :, cols], mate_s.at[c], mate_r.at[c], mate
        )

    def look_up():
        slots = slot_ref[...] - tr * slot_ref.shape[1]
        codes = jnp.broadcast_to(code_ref[...], (16, code_ref.shape[1]))
        high = (codes >> 7).astype(F32).astype(BF16)
        low = (codes & 127).astype(F32).astype(BF16)
        total = jnp.zeros((16, 1024), F32)
        for i in range(4):
            js = lax.broadcasted_iota(jnp.int32, (256, 1024), 0) + 256 * i
            hot = jnp.where(js == slots, 1.0, 0.0).astype(BF16)
            total = total + 128.0 * jnp.dot(high[:, 256 * i : 256 * (i + 1)], hot, preferred_element_type=F32)
            total = total + jnp.dot(low[:, 256 * i : 256 * (i + 1)], hot, preferred_element_type=F32)
        energy[0] = total[:8] / 1024.0
        flight["energy"] = send(energy.at[0], energy.at[1], en_s, en_r, mate)

    def weigh(o):
        e = energy[o]
        for k in range(16):
            order = jnp.full((8, 1024), freq_ref[k].astype(F32), F32)
            f = jnp.exp2(order * 0.5 - 4.0)
            weight[o, k] = 2.0 * e / (e * e + f * f) / trans

    def scale(o):
        for i, target in enumerate((z, z_mate, z_near, z_far)):
            target = lax.rem(target + 8, 8)
            rows = proj[o, target // 4].reshape(4, 8, 1024)
            for k in range(4):
                w = weight[o, lax.rem(target, 4) * 4 + k]
                scaled = (rows * w[None]).reshape(32, 1024)
                top = scaled.astype(BF16)
                at = slice(128 * i + 32 * k, 128 * i + 32 * (k + 1))
                lhs_hi[o, at, :] = top
                lhs_lo[o, at, :] = (scaled - top.astype(F32)).astype(BF16)

    project(0)
    project(1)
    add_core(0)
    project(2)
    pass1(0)
    add_core(1)
    project(3)
    look_up()
    close1(0)
    weigh(0)
    pass1(1)
    pass2(0)
    add_core(2)
    close1(1)
    close2(0)
    pass1(2)
    pass2(1)
    add_core(3)
    close3(0)
    flight["energy"].wait_recv()
    weigh(1)
    close1(2)
    close2(1)
    pass1(3)
    pass2(2)
    close3(1)
    close1(3)
    close2(2)
    pass2(3)
    close3(2)
    close2(3)
    close3(3)

    def spot(o, rel):
        return gath.at[o, SLOT[rel], core]

    def gather_send(o, rel, axis, way, rows, src=None):
        dy, dx = rel
        there = (dy, (dx - way) % 4) if axis else ((dy - way) % 4, dx)
        first, count = rows
        half = 0 if first == 0 else 1
        slot = SLOT[there]
        to = (xdev if axis else ydev)[way]
        src = spot(o, rel) if src is None else src
        flight["g", o, there, half] = send(
            src.at[pl.ds(first, count)],
            spot(o, there).at[pl.ds(first, count)],
            gath_s.at[o, slot, half],
            gath_r.at[o, slot, half],
            to,
        )

    def gather_core(o, rel, src=None):
        slot = SLOT[rel]
        flight["gc", o, rel] = send(
            spot(o, rel) if src is None else src,
            spot(o, rel),
            gcore_s.at[o, slot],
            gcore_r.at[o, slot],
            partner,
        )

    whole, halves = (0, 32), {1: (0, 16), -1: (16, 16)}

    def arrive(o, rel):
        flight["g", o, rel, 0].wait_recv()
        d_first, d_second = rel[::-1] if o == 0 else rel
        if d_second == 2 or (d_second == 0 and d_first == 2):
            flight["g", o, rel, 1].wait_recv()

    def spread(o, rel):
        arrive(o, rel)
        first = 1 - o
        d_first, d_second = rel[::-1] if first else rel
        if d_second == 0:
            if d_first in (1, 3):
                way = 1 if d_first == 3 else -1
                gather_send(o, rel, first, way, halves[way])
            for way in (1, -1):
                gather_send(o, rel, 1 - first, way, whole)
        elif d_second in (1, 3):
            way = 1 if d_second == 3 else -1
            gather_send(o, rel, 1 - first, way, halves[way])
        gather_core(o, rel)

    def begin(o):
        own = proj.at[o, par]
        first = 1 - o
        for axis in (first, 1 - first):
            for way in (1, -1):
                gather_send(o, (0, 0), axis, way, whole, src=own)
        gather_core(o, (0, 0), src=own)
        gath[o, 0, core] = own[...]

    def multiply(s):
        for o in (0, 1):
            for rel in SLOTS[2 * s : 2 * s + 2]:
                flight["gc", o, rel].wait_recv()
            rows = gath[o, 2 * s : 2 * s + 2].reshape(128, 1024)
            top = rows.astype(BF16)
            rhs_hi[o] = top
            rhs_lo[o] = (rows - top.astype(F32)).astype(BF16)
        dims = (((1,), (1,)), ((), ()))
        total = None
        for o in (0, 1):
            for a, b in ((lhs_hi, rhs_hi), (lhs_hi, rhs_lo), (lhs_lo, rhs_hi)):
                term = lax.dot_general(a[o], b[o], dims, preferred_element_type=F32)
                total = term if total is None else total + term
        sent[s] = total.reshape(4, 128, 128)
        for i, to in enumerate((mate, near, far)):
            flight["out", s, i] = send(sent.at[s, 1 + i], got.at[s, i], out_s.at[s, i], out_r.at[s, i], to)

    lane = lax.broadcasted_iota(jnp.int32, (128, 128), 1)

    def finish(s):
        for i in range(3):
            flight["out", s, i].wait_recv()
        same = sent[s, 0] + got[s, 2]
        other = got[s, 0] + got[s, 1]
        even = jnp.where(par == 0, same, other)
        odd = jnp.where(par == 0, other, same)
        for i, rel in enumerate(SLOTS[2 * s : 2 * s + 2]):
            if i == 0:
                full = jnp.where(lane < 64, even, pltpu.roll(odd, 64, 1))
            else:
                full = jnp.where(lane < 64, pltpu.roll(even, 64, 1), odd)
            block = lax.rem(y + rel[0], 4) * 4 + lax.rem(x + rel[1], 4)
            cols = pl.ds(pl.multiple_of(block * 128, 128), 128)
            out_ref[:, :, cols] = full.reshape(4, 32, 128)

    begin(0)
    scale(0)
    for c in range(NC):
        flight["mate", c].wait_recv()
    begin(1)
    scale(1)
    for rel in ((0, 1), (0, 3)):
        spread(0, rel)
        spread(1, rel[::-1])
    for rel in ((1, 0), (3, 0)):
        spread(0, rel)
        spread(1, rel[::-1])
    multiply(0)
    spread(0, (0, 2))
    spread(1, (2, 0))
    multiply(1)
    for rel in ((1, 1), (3, 1), (1, 3), (3, 3)):
        spread(0, rel)
        spread(1, rel[::-1])
    multiply(2)
    finish(0)
    multiply(3)
    finish(1)
    spread(0, (2, 0))
    spread(1, (0, 2))
    multiply(4)
    finish(2)
    for rel in ((1, 2), (3, 2)):
        spread(0, rel)
        spread(1, rel[::-1])
    for rel in ((2, 1), (2, 3)):
        spread(0, rel)
        spread(1, rel[::-1])
    multiply(5)
    finish(3)
    multiply(6)
    finish(4)
    spread(0, (2, 2))
    spread(1, (2, 2))
    multiply(7)
    for s in (5, 6, 7):
        finish(s)
    for copy in started:
        copy.wait_send()


def per_device(pair_density, basis, block_slot, energy_code, freq_order):
    tr_dev = pair_density.shape[1]
    vmem, dma = pltpu.VMEM, pltpu.SemaphoreType.DMA
    any_space = pl.BlockSpec(memory_space=pl.ANY)
    in_vmem = pl.BlockSpec(memory_space=pltpu.VMEM)
    scratch = [
        vmem((640, 1024), BF16),
        vmem((640, 2048), BF16),
        vmem((2048, 640), BF16),
        vmem((NC, 2, 4, 4, 2, 2, 32, 128), F32),
        vmem((NC, 2, 4, 4, 2, 32, 128), F32),
        vmem((NC, 2, 6, 4, 32, 128), F32),
        vmem((NC, 2, 4, 2, 32, 128), F32),
        vmem((NC, 2, 6, 32, 128), F32),
        vmem((NC, 2, 2, 32, 128), F32),
        vmem((NC, 2, 2, 32, 128), F32),
        vmem((2, 2, 32, 1024), F32),
        vmem((2, 8, 1024), F32),
        vmem((2, 16, 8, 1024), F32),
        vmem((2, 16, 2, 32, 1024), F32),
        vmem((2, 512, 1024), BF16),
        vmem((2, 512, 1024), BF16),
        vmem((2, 128, 1024), BF16),
        vmem((2, 128, 1024), BF16),
        vmem((NS, 4, 128, 128), F32),
        vmem((NS, 3, 128, 128), F32),
        dma((2,)),
        dma((NC,)), dma((NC,)),
        dma((NC, 2, 6)), dma((NC, 2, 6)),
        dma((NC, 2, 6)), dma((NC, 2, 6)),
        dma((NC,)), dma((NC,)),
        dma((NC,)), dma((NC,)),
        dma, dma,
        dma((2, 16, 2)), dma((2, 16, 2)),
        dma((2, 16)), dma((2, 16)),
        dma((NS, 3)), dma((NS, 3)),
    ]
    return pl.pallas_call(
        functools.partial(kernel, float(tr_dev * lax.axis_size("tr"))),
        out_shape=jax.ShapeDtypeStruct((4, 32, 2048), F32),
        in_specs=[pl.BlockSpec(memory_space=pltpu.SMEM), in_vmem, in_vmem, any_space, any_space],
        out_specs=in_vmem,
        scratch_shapes=scratch,
        compiler_params=pltpu.CompilerParams(
            collective_id=0, has_side_effects=True, vmem_limit_bytes=60 * 2**20
        ),
        name="polarizability",
    )(
        freq_order,
        block_slot.reshape(1, tr_dev),
        energy_code.reshape(1, tr_dev),
        pair_density,
        basis,
    )


def solution(mesh):
    placed = (P("pw", "tr"), P("pw", None), P("tr"), P("tr"), P())
    return jax.shard_map(
        per_device, mesh=mesh, in_specs=placed, out_specs=P("tr", "pw", None), check_vma=False
    )
```

```python
import functools

import jax
import jax.numpy as jnp
from jax import lax
from jax.experimental import pallas as pl
from jax.experimental.pallas import tpu as pltpu
from jax.sharding import PartitionSpec as P

F32 = jnp.float32
BF16 = jnp.bfloat16
MESH = pl.DeviceIdType.MESH

SLOTS = [
    (0, 0), (0, 1), (0, 3), (1, 0),
    (3, 0), (1, 1), (1, 3), (3, 1),
    (3, 3), (0, 2), (2, 0), (1, 2),
    (3, 2), (2, 1), (2, 3), (2, 2),
]
SLOT = {rel: i for i, rel in enumerate(SLOTS)}

ORDER = [
    ("lookup",), ("weigh", 0), ("add", 0), ("weigh", 1), ("pass1", 0), ("add", 1), ("close1", 0),
    ("pass1", 1), ("add", 2), ("close2", 0), ("close1", 1), ("pass1", 2), ("add", 3), ("close2", 1),
    ("close3", 0), ("close1", 2), ("pass1", 3), ("close2", 2), ("close3", 1), ("begin", 0, 0), ("close1", 3),
    ("scale", 0, 0), ("spread", 0, 0, (0, 3)), ("spread", 0, 0, (0, 1)), ("spread", 0, 0, (1, 0)),
    ("spread", 0, 0, (3, 0)), ("close2", 3), ("close3", 2), ("begin", 0, 1), ("scale", 0, 1),
    ("spread", 0, 0, (0, 2)), ("spread", 0, 0, (3, 3)), ("spread", 0, 0, (1, 3)), ("spread", 0, 0, (3, 1)),
    ("spread", 0, 0, (1, 1)), ("spread", 0, 0, (2, 0)), ("spread", 0, 1, (0, 3)), ("spread", 0, 1, (0, 1)),
    ("spread", 0, 1, (3, 0)), ("spread", 0, 1, (1, 0)), ("convert", 0, 0), ("close3", 3),
    ("spread", 0, 0, (1, 2)), ("spread", 0, 0, (3, 2)), ("spread", 0, 1, (0, 2)), ("begin", 1, 0),
    ("spread", 0, 0, (2, 3)), ("scale", 1, 0), ("multiply", 0, 0, 0), ("spread", 0, 0, (2, 1)),
    ("spread", 0, 1, (2, 0)), ("spread", 0, 1, (3, 1)), ("spread", 0, 1, (3, 3)), ("spread", 0, 0, (2, 2)),
    ("spread", 0, 1, (1, 3)), ("spread", 0, 1, (1, 1)), ("begin", 1, 1), ("scale", 1, 1),
    ("multiply", 1, 0, 0), ("spread", 1, 0, (0, 1)), ("spread", 1, 0, (0, 3)), ("spread", 1, 0, (1, 0)),
    ("spread", 1, 0, (3, 0)), ("convert", 0, 1), ("multiply", 0, 0, 1), ("spread", 0, 1, (2, 1)),
    ("spread", 0, 1, (2, 3)), ("spread", 0, 1, (3, 2)), ("spread", 1, 1, (1, 0)), ("spread", 1, 1, (3, 0)),
    ("multiply", 1, 0, 1), ("spread", 0, 1, (1, 2)), ("spread", 1, 0, (3, 1)), ("spread", 1, 0, (1, 1)),
    ("spread", 1, 1, (0, 3)), ("spread", 1, 1, (0, 1)), ("convert", 0, 2), ("multiply", 0, 0, 2),
    ("spread", 0, 1, (2, 2)), ("spread", 1, 0, (0, 2)), ("spread", 1, 0, (2, 0)), ("spread", 1, 0, (1, 3)),
    ("spread", 1, 0, (3, 3)), ("multiply", 1, 0, 2), ("spread", 1, 1, (2, 0)), ("spread", 1, 0, (2, 1)),
    ("spread", 1, 1, (1, 1)), ("spread", 1, 1, (1, 3)), ("convert", 0, 3), ("multiply", 0, 0, 3),
    ("spread", 1, 1, (3, 1)), ("spread", 1, 1, (3, 3)), ("multiply", 1, 0, 3), ("spread", 1, 0, (1, 2)),
    ("spread", 1, 0, (3, 2)), ("spread", 1, 0, (2, 3)), ("spread", 1, 1, (0, 2)), ("convert", 1, 0),
    ("multiply", 0, 1, 0), ("spread", 1, 1, (1, 2)), ("spread", 1, 1, (2, 1)), ("spread", 1, 1, (2, 3)),
    ("convert", 1, 1), ("spread", 1, 1, (3, 2)), ("multiply", 0, 1, 1), ("spread", 1, 0, (2, 2)),
    ("convert", 1, 2), ("multiply", 0, 1, 2), ("spread", 1, 1, (2, 2)), ("multiply", 1, 1, 0),
    ("multiply", 1, 1, 1), ("convert", 1, 3), ("multiply", 0, 1, 3), ("multiply", 1, 1, 2),
    ("multiply", 1, 1, 3), ("finish", 0, 0), ("finish", 0, 1), ("finish", 0, 2), ("finish", 1, 0),
    ("finish", 1, 1), ("finish", 0, 3), ("finish", 1, 2), ("finish", 1, 3),
]


def device(y, x, z, core):
    y, x, z = lax.rem(y + 4, 4), lax.rem(x + 4, 4), lax.rem(z + 8, 8)
    return ((y * 4 + x) * 2 + z // 4) * 2 + core, lax.rem(z, 4)


def kernel(
    trans,
    freq_ref, slot_ref, code_ref, pair_hbm, basis_hbm, out_ref,
    pair, basis, basis_t, part, mine, ring1, ring1_sum, ring2, ring2_sum, zrecv,
    proj, energy, weight, gath, lhs_hi, lhs_lo, rhs_hi, rhs_lo, sent, got,
    load_sem, core_s, core_r, ring1_s, ring1_r, ring2_s, ring2_r, z_s, z_r,
    mate_s, mate_r, en_s, en_r, gath_s, gath_r, gcore_s, gcore_r, out_s, out_r,
):
    pw, tr = lax.axis_index("pw"), lax.axis_index("tr")
    core, zh = lax.rem(pw, 2), lax.rem(pw // 2, 2)
    x, y = lax.rem(pw // 4, 4), pw // 16
    z = zh * 4 + tr
    par = lax.rem(z, 2)
    away = 1 - 2 * par

    partner = device(y, x, z, 1 - core)
    ydev = {d: device(y + d, x, z, core) for d in (1, -1, 2)}
    xdev = {d: device(y, x + d, z, core) for d in (1, -1, 2)}
    opposite = device(y, x, z + 4, core)
    z_mate, z_near, z_far = z + away, z - away, z + 2 * away
    mate, near = device(y, x, z_mate, core), device(y, x, z_near, core)
    far, far_from = device(y, x, z_far, core), device(y, x, z - 2 * away, core)

    load_pair = pltpu.make_async_copy(pair_hbm, pair, load_sem.at[0])
    load_basis = pltpu.make_async_copy(basis_hbm, basis, load_sem.at[1])
    load_basis.start()
    load_pair.start()

    barrier = pltpu.get_barrier_semaphore()
    peers = (partner, *ydev.values(), *xdev.values(), opposite, mate, near, far, far_from)
    for peer in peers:
        pl.semaphore_signal(barrier, inc=1, device_id=peer, device_id_type=MESH)

    started = []
    flight = {}

    def send(key, src, dst, ssem, rsem, to):
        copy = pltpu.make_async_remote_copy(
            src_ref=src, dst_ref=dst, send_sem=ssem, recv_sem=rsem, device_id=to, device_id_type=MESH
        )
        copy.start()
        started.append(copy)
        flight[key] = copy

    load_basis.wait()
    basis_t[...] = basis[...].T
    load_pair.wait()

    for u in (0, 1):
        cols = pair[:, 512 * u : 512 * (u + 1)]

        @pl.loop(0, 4)
        def _(i):
            rows = basis_t[pl.ds(pl.multiple_of(i * 512, 512), 512), :]
            block = jnp.dot(rows, cols, preferred_element_type=F32)
            for j in range(4):
                piece = block[128 * j : 128 * (j + 1)]
                part[u, 0, i, j] = piece[:, :256].reshape(2, 2, 32, 256)
                part[u, 1, j, i] = piece[:, 256:].reshape(2, 2, 32, 256)

    pl.semaphore_wait(barrier, len(peers))

    place = ((y, x), (x, y))
    line = ((ydev, xdev), (xdev, ydev))

    for c in range(4):
        j, u = divmod(c, 2)
        send(
            ("core", c),
            part.at[u, :, :, :, :, 1 - core, pl.ds(16 * j, 16)],
            mine.at[c],
            core_s.at[c],
            core_r.at[c],
            partner,
        )

    def add(c):
        j, u = divmod(c, 2)
        flight["core", c].wait_recv()

        @pl.loop(0, 4)
        def _(i):
            mine[c, :, i] = mine[c, :, i] + part[u, :, i, :, :, core, 16 * j : 16 * (j + 1)]

        for order in (0, 1):
            at, to = place[order][0], line[order][0]
            ahead, behind, across = (lax.rem(at + d, 4) for d in (1, 3, 2))
            pieces = ((across, 0, 1), (across, 1, -1), (ahead, 1, 1), (behind, 0, -1))
            for i, (p, half, way) in enumerate(pieces):
                send(
                    ("r1", c, order, i),
                    mine.at[c, order, p, :, half],
                    ring1.at[c, order, i],
                    ring1_s.at[c, order, i],
                    ring1_r.at[c, order, i],
                    to[way],
                )

    def pass1(c):
        for order in (0, 1):
            at, to = place[order][0], line[order][0]
            for i, (p, way) in enumerate(((lax.rem(at + 1, 4), 1), (lax.rem(at + 3, 4), -1))):
                flight["r1", c, order, i].wait_recv()
                ring1[c, order, i] = ring1[c, order, i] + mine[c, order, p, :, i]
                send(
                    ("r1", c, order, 4 + i),
                    ring1.at[c, order, i],
                    ring1.at[c, order, 4 + i],
                    ring1_s.at[c, order, 4 + i],
                    ring1_r.at[c, order, 4 + i],
                    to[way],
                )

    def close1(c):
        for order in (0, 1):
            at = place[order][0]
            for i in (2, 3, 4, 5):
                flight["r1", c, order, i].wait_recv()
            for half, i, k in ((0, 3, 4), (1, 2, 5)):
                ring1_sum[c, order, :, half] = mine[c, order, at, :, half] + ring1[c, order, i] + ring1[c, order, k]
            at, to = place[order][1], line[order][1]
            for i, way in enumerate((2, 1, -1)):
                send(
                    ("r2", c, order, i),
                    ring1_sum.at[c, order, lax.rem(at + way + 4, 4)],
                    ring2.at[c, order, i],
                    ring2_s.at[c, order, i],
                    ring2_r.at[c, order, i],
                    to[way],
                )

    def close2(c):
        for order in (0, 1):
            at = place[order][1]
            for i in range(3):
                flight["r2", c, order, i].wait_recv()
            ring2_sum[c, order] = (ring1_sum[c, order, at] + ring2[c, order, 0]) + (
                ring2[c, order, 1] + ring2[c, order, 2]
            )
        send(("z", c), ring2_sum.at[c], zrecv.at[c], z_s.at[c], z_r.at[c], opposite)

    def close3(c):
        j, u = divmod(c, 2)
        flight["z", c].wait_recv()
        for order in (0, 1):
            first = 512 * u + 256 * order
            proj[0, j, :, :, first : first + 256] = ring2_sum[c, order] + zrecv[c, order]
        cols = pl.ds(512 * u, 512)
        send(
            ("mate", c),
            proj.at[0, j, :, :, cols],
            proj.at[1, j, :, :, cols],
            mate_s.at[c],
            mate_r.at[c],
            mate,
        )

    def lookup():
        slots = slot_ref[...] - tr * slot_ref.shape[1]
        codes = jnp.broadcast_to(code_ref[...], (16, code_ref.shape[1]))
        high = (codes >> 7).astype(F32).astype(BF16)
        low = (codes & 127).astype(F32).astype(BF16)
        total = jnp.zeros((16, 1024), F32)
        for i in range(4):
            js = lax.broadcasted_iota(jnp.int32, (256, 1024), 0) + 256 * i
            hot = jnp.where(js == slots, 1.0, 0.0).astype(BF16)
            total = total + 128.0 * jnp.dot(high[:, 256 * i : 256 * (i + 1)], hot, preferred_element_type=F32)
            total = total + jnp.dot(low[:, 256 * i : 256 * (i + 1)], hot, preferred_element_type=F32)
        energy[0] = total[:8] / 1024.0
        send("energy", energy.at[0], energy.at[1], en_s, en_r, mate)

    def weigh(o):
        if o == 1:
            flight["energy"].wait_recv()
        e = energy[o]
        for k in range(16):
            order = jnp.full((8, 1024), freq_ref[k].astype(F32), F32)
            f = jnp.exp2(order * 0.5 - 4.0)
            weight[o, k] = 2.0 * e / (e * e + f * f) / trans

    def scale(j, o):
        for i, target in enumerate((z, z_mate, z_near, z_far)):
            target = lax.rem(target + 8, 8)
            rows = proj[o, j, target // 4].reshape(2, 8, 1024)
            for k in range(4):
                w = weight[o, lax.rem(target, 4) * 4 + k]
                scaled = (rows * w[None]).reshape(16, 1024)
                top = scaled.astype(BF16)
                at = slice(64 * i + 16 * k, 64 * i + 16 * (k + 1))
                lhs_hi[j, o, at, :] = top
                lhs_lo[j, o, at, :] = (scaled - top.astype(F32)).astype(BF16)

    whole, halves = (0, 16), {1: (0, 8), -1: (8, 8)}

    def pass_on(j, o, rel, axis, way, rows, src):
        dy, dx = rel
        there = (dy, (dx - way) % 4) if axis else ((dy - way) % 4, dx)
        slot, half, rows = SLOT[there], int(rows[0] > 0), pl.ds(*rows)
        send(
            ("g", j, o, there, half),
            src.at[rows],
            gath.at[j, o, slot, core, rows],
            gath_s.at[j, o, slot, half],
            gath_r.at[j, o, slot, half],
            (xdev if axis else ydev)[way],
        )

    def cross(j, o, rel, src):
        slot = SLOT[rel]
        send(
            ("gc", j, o, rel), src, gath.at[j, o, slot, core], gcore_s.at[j, o, slot], gcore_r.at[j, o, slot], partner
        )

    def begin(j, o):
        if o == 1:
            for u in (0, 1):
                flight["mate", 2 * j + u].wait_recv()
        own = proj.at[o, j, par]
        for axis in (1 - o, o):
            for way in (1, -1):
                pass_on(j, o, (0, 0), axis, way, whole, own)
        cross(j, o, (0, 0), own)
        gath[j, o, 0, core] = own[...]

    def spread(j, o, rel):
        first, second = rel if o else rel[::-1]
        flight["g", j, o, rel, 0].wait_recv()
        if second == 2 or (second == 0 and first == 2):
            flight["g", j, o, rel, 1].wait_recv()
        src = gath.at[j, o, SLOT[rel], core]
        ways = {3: 1, 1: -1}
        if second == 0:
            if first != 2:
                pass_on(j, o, rel, 1 - o, ways[first], halves[ways[first]], src)
            for way in (1, -1):
                pass_on(j, o, rel, o, way, whole, src)
        elif second != 2:
            pass_on(j, o, rel, o, ways[second], halves[ways[second]], src)
        cross(j, o, rel, src)

    def convert(j, s):
        for o in (0, 1):
            for i, rel in enumerate(SLOTS[4 * s : 4 * s + 4]):
                flight["gc", j, o, rel].wait_recv()
                for k in (0, 1):
                    spot = 2 * (2 * (i % 2) + k) + (j if i < 2 else 1 - j)
                    rows = gath[j, o, 4 * s + i, k]
                    top = rows.astype(BF16)
                    at = slice(16 * spot, 16 * (spot + 1))
                    rhs_hi[j, s, o, at, :] = top
                    rhs_lo[j, s, o, at, :] = (rows - top.astype(F32)).astype(BF16)

    def multiply(n, j, s):
        dims = (((1,), (1,)), ((), ()))
        total = None
        for o in (0, 1):
            for a, b in ((lhs_hi, rhs_hi), (lhs_hi, rhs_lo), (lhs_lo, rhs_hi)):
                term = lax.dot_general(a[n, o], b[j, s, o], dims, preferred_element_type=F32)
                total = term if total is None else total + term
        sent[n, j, s] = total.reshape(4, 64, 128)
        for i, to in enumerate((mate, near, far)):
            send(
                ("out", n, j, s, i),
                sent.at[n, j, s, 1 + i],
                got.at[n, j, s, i],
                out_s.at[n, j, s, i],
                out_r.at[n, j, s, i],
                to,
            )

    lane = lax.broadcasted_iota(jnp.int32, (64, 128), 1)
    left, first_half = lane < 64, lax.rem(lane // 16, 2) == 0

    def finish(n, s):
        parts = []
        for j in (0, 1):
            for i in range(3):
                flight["out", n, j, s, i].wait_recv()
            same = sent[n, j, s, 0] + got[n, j, s, 2]
            other = got[n, j, s, 0] + got[n, j, s, 1]
            parts.append((jnp.where(par == 0, same, other), jnp.where(par == 0, other, same)))
        for i in (0, 1):
            merged = []
            for low, high in zip(*parts):
                if i:
                    low, high = pltpu.roll(low, 112, 1), pltpu.roll(high, 16, 1)
                merged.append(jnp.where(first_half, low, high))
            even, odd = merged
            fulls = (
                jnp.where(left, even, pltpu.roll(odd, 64, 1)),
                jnp.where(left, pltpu.roll(even, 64, 1), odd),
            )
            for full, rel in zip(fulls, SLOTS[4 * s + 2 * i : 4 * s + 2 * i + 2]):
                block = lax.rem(y + rel[0], 4) * 4 + lax.rem(x + rel[1], 4)
                cols = pl.ds(pl.multiple_of(block * 128, 128), 128)
                out_ref[:, 16 * n : 16 * (n + 1), cols] = full.reshape(4, 16, 128)

    steps = dict(
        add=add, pass1=pass1, close1=close1, close2=close2, close3=close3, lookup=lookup, weigh=weigh, scale=scale,
        begin=begin, spread=spread, convert=convert, multiply=multiply, finish=finish,
    )
    for name, *args in ORDER:
        steps[name](*args)
    for copy in started:
        copy.wait_send()


def per_device(pair_density, basis, block_slot, energy_code, freq_order):
    tr_dev = pair_density.shape[1]
    vmem, dma = pltpu.VMEM, pltpu.SemaphoreType.DMA
    any_space = pl.BlockSpec(memory_space=pl.ANY)
    in_vmem = pl.BlockSpec(memory_space=pltpu.VMEM)
    scratch = [
        vmem((640, 1024), BF16),
        vmem((640, 2048), BF16),
        vmem((2048, 640), BF16),
        vmem((2, 2, 4, 4, 2, 2, 32, 256), F32),
        vmem((4, 2, 4, 4, 2, 16, 256), F32),
        vmem((4, 2, 6, 4, 16, 256), F32),
        vmem((4, 2, 4, 2, 16, 256), F32),
        vmem((4, 2, 3, 2, 16, 256), F32),
        vmem((4, 2, 2, 16, 256), F32),
        vmem((4, 2, 2, 16, 256), F32),
        vmem((2, 2, 2, 16, 1024), F32),
        vmem((2, 8, 1024), F32),
        vmem((2, 16, 8, 1024), F32),
        vmem((2, 2, 16, 2, 16, 1024), F32),
        vmem((2, 2, 256, 1024), BF16),
        vmem((2, 2, 256, 1024), BF16),
        vmem((2, 4, 2, 128, 1024), BF16),
        vmem((2, 4, 2, 128, 1024), BF16),
        vmem((2, 2, 4, 4, 64, 128), F32),
        vmem((2, 2, 4, 3, 64, 128), F32),
        dma((2,)),
        dma((4,)), dma((4,)),
        dma((4, 2, 6)), dma((4, 2, 6)),
        dma((4, 2, 3)), dma((4, 2, 3)),
        dma((4,)), dma((4,)),
        dma((4,)), dma((4,)),
        dma, dma,
        dma((2, 2, 16, 2)), dma((2, 2, 16, 2)),
        dma((2, 2, 16)), dma((2, 2, 16)),
        dma((2, 2, 4, 3)), dma((2, 2, 4, 3)),
    ]
    return pl.pallas_call(
        functools.partial(kernel, float(tr_dev * lax.axis_size("tr"))),
        out_shape=jax.ShapeDtypeStruct((4, 32, 2048), F32),
        in_specs=[pl.BlockSpec(memory_space=pltpu.SMEM), in_vmem, in_vmem, any_space, any_space],
        out_specs=in_vmem,
        scratch_shapes=scratch,
        compiler_params=pltpu.CompilerParams(
            collective_id=0, has_side_effects=True, vmem_limit_bytes=60 * 2**20
        ),
        name="polarizability",
    )(
        freq_order,
        block_slot.reshape(1, tr_dev),
        energy_code.reshape(1, tr_dev),
        pair_density,
        basis,
    )


def solution(mesh):
    placed = (P("pw", "tr"), P("pw", None), P("tr"), P("tr"), P())
    return jax.shard_map(
        per_device, mesh=mesh, in_specs=placed, out_specs=P("tr", "pw", None), check_vma=False
    )
```

```python
import functools

import jax
import jax.numpy as jnp
from jax import lax
from jax.experimental import pallas as pl
from jax.experimental.pallas import tpu as pltpu
from jax.sharding import PartitionSpec as P

F32 = jnp.float32
BF16 = jnp.bfloat16
MESH = pl.DeviceIdType.MESH

SLOTS = [
    (0, 0), (0, 1), (0, 3), (1, 0),
    (3, 0), (1, 1), (1, 3), (3, 1),
    (3, 3), (0, 2), (2, 0), (1, 2),
    (3, 2), (2, 1), (2, 3), (2, 2),
]
SLOT = {rel: i for i, rel in enumerate(SLOTS)}

ORDER = [
    ("project", 0), ("project", 1), ("project", 2), ("add", 0), ("project", 3), ("lookup",), ("weigh", 0),
    ("pass1", 0), ("add", 1), ("weigh", 1), ("close1", 0), ("pass1", 1), ("add", 2), ("close2", 0),
    ("close1", 1), ("pass1", 2), ("add", 3), ("close2", 1), ("close1", 2), ("pass1", 3), ("close3", 0),
    ("close2", 2), ("close1", 3), ("close3", 1), ("scale", 0, 0), ("begin", 0, 0), ("close2", 3),
    ("spread", 0, 0, (0, 3)), ("spread", 0, 0, (3, 0)), ("begin", 0, 1), ("scale", 0, 1),
    ("spread", 0, 0, (0, 1)), ("spread", 0, 0, (1, 0)), ("close3", 2), ("spread", 0, 0, (3, 3)),
    ("spread", 0, 0, (1, 3)), ("spread", 0, 1, (0, 1)), ("spread", 0, 1, (0, 3)), ("spread", 0, 0, (0, 2)),
    ("spread", 0, 1, (1, 0)), ("spread", 0, 1, (3, 0)), ("close3", 3), ("begin", 1, 0), ("convert", 0, 0),
    ("scale", 1, 0), ("spread", 0, 0, (2, 0)), ("spread", 0, 0, (3, 1)), ("spread", 0, 0, (1, 1)),
    ("multiply", 0, 0, 0), ("spread", 0, 1, (0, 2)), ("spread", 0, 0, (2, 3)), ("spread", 0, 1, (1, 3)),
    ("spread", 0, 0, (1, 2)), ("spread", 0, 1, (1, 1)), ("spread", 0, 0, (3, 2)), ("spread", 0, 1, (2, 0)),
    ("begin", 1, 1), ("spread", 0, 1, (3, 3)), ("spread", 0, 1, (3, 1)), ("scale", 1, 1),
    ("multiply", 1, 0, 0), ("convert", 0, 1), ("multiply", 1, 0, 1), ("spread", 0, 0, (2, 1)),
    ("spread", 0, 1, (1, 2)), ("spread", 1, 0, (1, 0)), ("spread", 1, 0, (0, 3)), ("spread", 1, 0, (3, 0)),
    ("spread", 1, 0, (0, 1)), ("spread", 0, 0, (2, 2)), ("multiply", 0, 0, 1), ("spread", 0, 1, (2, 1)),
    ("spread", 0, 1, (2, 3)), ("spread", 1, 1, (1, 0)), ("convert", 0, 2), ("multiply", 1, 0, 2),
    ("spread", 0, 1, (3, 2)), ("spread", 1, 1, (0, 3)), ("spread", 1, 1, (0, 1)), ("spread", 1, 1, (3, 0)),
    ("multiply", 0, 0, 2), ("spread", 1, 0, (0, 2)), ("spread", 1, 0, (3, 3)), ("convert", 1, 0),
    ("spread", 1, 0, (1, 3)), ("multiply", 1, 1, 0), ("spread", 0, 1, (2, 2)), ("spread", 1, 0, (2, 0)),
    ("spread", 1, 0, (1, 1)), ("spread", 1, 1, (1, 1)), ("spread", 1, 1, (1, 3)), ("spread", 1, 0, (3, 1)),
    ("multiply", 0, 1, 0), ("spread", 1, 1, (2, 0)), ("spread", 1, 1, (0, 2)), ("convert", 0, 3),
    ("multiply", 1, 0, 3), ("spread", 1, 0, (3, 2)), ("spread", 1, 1, (3, 3)), ("spread", 1, 1, (3, 1)),
    ("spread", 1, 0, (1, 2)), ("spread", 1, 0, (2, 3)), ("multiply", 0, 0, 3), ("spread", 1, 1, (1, 2)),
    ("spread", 1, 0, (2, 1)), ("convert", 1, 1), ("multiply", 1, 1, 1), ("spread", 1, 1, (2, 3)),
    ("spread", 1, 1, (2, 1)), ("multiply", 0, 1, 1), ("spread", 1, 1, (3, 2)), ("spread", 1, 0, (2, 2)),
    ("convert", 1, 2), ("multiply", 1, 1, 2), ("multiply", 0, 1, 2), ("spread", 1, 1, (2, 2)),
    ("finish", 0, 0), ("finish", 1, 0), ("convert", 1, 3), ("multiply", 1, 1, 3), ("multiply", 0, 1, 3),
    ("finish", 1, 1), ("finish", 0, 1), ("finish", 1, 2), ("finish", 0, 2), ("finish", 1, 3),
    ("finish", 0, 3),
]


def device(y, x, z, core):
    y, x, z = lax.rem(y + 4, 4), lax.rem(x + 4, 4), lax.rem(z + 8, 8)
    return ((y * 4 + x) * 2 + z // 4) * 2 + core, lax.rem(z, 4)


def kernel(
    trans,
    freq_ref, slot_ref, code_ref, pair_hbm, basis_hbm, out_ref,
    pair, basis, basis_t, part, mine, ring1, ring1_sum, ring2, ring2_sum, zrecv,
    proj, energy, weight, gath, lhs_hi, lhs_lo, rhs_hi, rhs_lo, sent, got,
    load_sem, core_s, core_r, ring1_s, ring1_r, ring2_s, ring2_r, z_s, z_r,
    mate_s, mate_r, en_s, en_r, gath_s, gath_r, gcore_s, gcore_r, out_s, out_r,
):
    pw, tr = lax.axis_index("pw"), lax.axis_index("tr")
    core, zh = lax.rem(pw, 2), lax.rem(pw // 2, 2)
    x, y = lax.rem(pw // 4, 4), pw // 16
    z = zh * 4 + tr
    par = lax.rem(z, 2)
    away = 1 - 2 * par

    partner = device(y, x, z, 1 - core)
    ydev = {d: device(y + d, x, z, core) for d in (1, -1, 2)}
    xdev = {d: device(y, x + d, z, core) for d in (1, -1, 2)}
    opposite = device(y, x, z + 4, core)
    z_mate, z_near, z_far = z + away, z - away, z + 2 * away
    mate, near = device(y, x, z_mate, core), device(y, x, z_near, core)
    far, far_from = device(y, x, z_far, core), device(y, x, z - 2 * away, core)

    load_pair = pltpu.make_async_copy(pair_hbm, pair, load_sem.at[0])
    load_basis = pltpu.make_async_copy(basis_hbm, basis, load_sem.at[1])
    load_basis.start()
    load_pair.start()

    barrier = pltpu.get_barrier_semaphore()
    peers = (partner, *ydev.values(), *xdev.values(), opposite, mate, near, far, far_from)
    for peer in peers:
        pl.semaphore_signal(barrier, inc=1, device_id=peer, device_id_type=MESH)

    started = []
    flight = {}

    def send(key, src, dst, ssem, rsem, to):
        copy = pltpu.make_async_remote_copy(
            src_ref=src, dst_ref=dst, send_sem=ssem, recv_sem=rsem, device_id=to, device_id_type=MESH
        )
        copy.start()
        started.append(copy)
        flight[key] = copy

    load_basis.wait()
    turned = basis[...].T.reshape(64, 2, 16, 640)
    for j in (0, 1):
        basis_t[j] = turned[:, j].reshape(1024, 640)
    load_pair.wait()

    place = ((y, x), (x, y))
    line = ((ydev, xdev), (xdev, ydev))

    def project(c):
        j, u = divmod(c, 2)
        cols = pair[:, 512 * u : 512 * (u + 1)]

        @pl.loop(0, 4)
        def _(i):
            rows = basis_t[j, pl.ds(pl.multiple_of(i * 256, 256), 256), :]
            block = jnp.dot(rows, cols, preferred_element_type=F32)
            for k in range(4):
                piece = block[64 * k : 64 * (k + 1)]
                part[c, 0, i, k] = piece[:, :256].reshape(2, 2, 16, 256)
                part[c, 1, k, i] = piece[:, 256:].reshape(2, 2, 16, 256)

        if c == 0:
            pl.semaphore_wait(barrier, len(peers))
        send(
            ("core", c), part.at[c, :, :, :, :, 1 - core], mine.at[c], core_s.at[c], core_r.at[c], partner
        )

    def add(c):
        flight["core", c].wait_recv()

        @pl.loop(0, 4)
        def _(i):
            mine[c, :, i] = mine[c, :, i] + part[c, :, i, :, :, core]

        for order in (0, 1):
            at, to = place[order][0], line[order][0]
            ahead, behind, across = (lax.rem(at + d, 4) for d in (1, 3, 2))
            pieces = ((across, 0, 1), (across, 1, -1), (ahead, 1, 1), (behind, 0, -1))
            for i, (p, half, way) in enumerate(pieces):
                send(
                    ("r1", c, order, i),
                    mine.at[c, order, p, :, half],
                    ring1.at[c, order, i],
                    ring1_s.at[c, order, i],
                    ring1_r.at[c, order, i],
                    to[way],
                )

    def pass1(c):
        for order in (0, 1):
            at, to = place[order][0], line[order][0]
            for i, (p, way) in enumerate(((lax.rem(at + 1, 4), 1), (lax.rem(at + 3, 4), -1))):
                flight["r1", c, order, i].wait_recv()
                ring1[c, order, i] = ring1[c, order, i] + mine[c, order, p, :, i]
                send(
                    ("r1", c, order, 4 + i),
                    ring1.at[c, order, i],
                    ring1.at[c, order, 4 + i],
                    ring1_s.at[c, order, 4 + i],
                    ring1_r.at[c, order, 4 + i],
                    to[way],
                )

    def close1(c):
        for order in (0, 1):
            at = place[order][0]
            for i in (2, 3, 4, 5):
                flight["r1", c, order, i].wait_recv()
            for half, i, k in ((0, 3, 4), (1, 2, 5)):
                ring1_sum[c, order, :, half] = mine[c, order, at, :, half] + ring1[c, order, i] + ring1[c, order, k]
            at, to = place[order][1], line[order][1]
            for i, way in enumerate((2, 1, -1)):
                send(
                    ("r2", c, order, i),
                    ring1_sum.at[c, order, lax.rem(at + way + 4, 4)],
                    ring2.at[c, order, i],
                    ring2_s.at[c, order, i],
                    ring2_r.at[c, order, i],
                    to[way],
                )

    def close2(c):
        for order in (0, 1):
            at = place[order][1]
            for i in range(3):
                flight["r2", c, order, i].wait_recv()
            ring2_sum[c, order] = (ring1_sum[c, order, at] + ring2[c, order, 0]) + (
                ring2[c, order, 1] + ring2[c, order, 2]
            )
        send(("z", c), ring2_sum.at[c], zrecv.at[c], z_s.at[c], z_r.at[c], opposite)

    def close3(c):
        j, u = divmod(c, 2)
        flight["z", c].wait_recv()
        for order in (0, 1):
            first = 512 * u + 256 * order
            proj[0, j, :, :, first : first + 256] = ring2_sum[c, order] + zrecv[c, order]
        cols = pl.ds(512 * u, 512)
        send(
            ("mate", c),
            proj.at[0, j, :, :, cols],
            proj.at[1, j, :, :, cols],
            mate_s.at[c],
            mate_r.at[c],
            mate,
        )

    def lookup():
        slots = slot_ref[...] - tr * slot_ref.shape[1]
        codes = jnp.broadcast_to(code_ref[...], (16, code_ref.shape[1]))
        high = (codes >> 7).astype(F32).astype(BF16)
        low = (codes & 127).astype(F32).astype(BF16)
        total = jnp.zeros((16, 1024), F32)
        for i in range(4):
            js = lax.broadcasted_iota(jnp.int32, (256, 1024), 0) + 256 * i
            hot = jnp.where(js == slots, 1.0, 0.0).astype(BF16)
            total = total + 128.0 * jnp.dot(high[:, 256 * i : 256 * (i + 1)], hot, preferred_element_type=F32)
            total = total + jnp.dot(low[:, 256 * i : 256 * (i + 1)], hot, preferred_element_type=F32)
        energy[0] = total[:8] / 1024.0
        send("energy", energy.at[0], energy.at[1], en_s, en_r, mate)

    def weigh(o):
        if o == 1:
            flight["energy"].wait_recv()
        e = energy[o]
        for k in range(16):
            order = jnp.full((8, 1024), freq_ref[k].astype(F32), F32)
            f = jnp.exp2(order * 0.5 - 4.0)
            weight[o, k] = 2.0 * e / (e * e + f * f) / trans

    def scale(j, o):
        for i, target in enumerate((z, z_mate, z_near, z_far)):
            target = lax.rem(target + 8, 8)
            rows = proj[o, j, target // 4].reshape(2, 8, 1024)
            for k in range(4):
                w = weight[o, lax.rem(target, 4) * 4 + k]
                scaled = (rows * w[None]).reshape(16, 1024)
                top = scaled.astype(BF16)
                at = slice(64 * i + 16 * k, 64 * i + 16 * (k + 1))
                lhs_hi[j, o, at, :] = top
                lhs_lo[j, o, at, :] = (scaled - top.astype(F32)).astype(BF16)

    whole, halves = (0, 16), {1: (0, 8), -1: (8, 8)}

    def pass_on(j, o, rel, axis, way, rows, src):
        dy, dx = rel
        there = (dy, (dx - way) % 4) if axis else ((dy - way) % 4, dx)
        slot, half, rows = SLOT[there], int(rows[0] > 0), pl.ds(*rows)
        send(
            ("g", j, o, there, half),
            src.at[rows],
            gath.at[j, o, slot, core, rows],
            gath_s.at[j, o, slot, half],
            gath_r.at[j, o, slot, half],
            (xdev if axis else ydev)[way],
        )

    def cross(j, o, rel, src):
        slot = SLOT[rel]
        send(
            ("gc", j, o, rel), src, gath.at[j, o, slot, core], gcore_s.at[j, o, slot], gcore_r.at[j, o, slot], partner
        )

    def begin(j, o):
        if o == 1:
            for u in (0, 1):
                flight["mate", 2 * j + u].wait_recv()
        own = proj.at[o, j, par]
        for axis in (1 - o, o):
            for way in (1, -1):
                pass_on(j, o, (0, 0), axis, way, whole, own)
        cross(j, o, (0, 0), own)
        gath[j, o, 0, core] = own[...]

    def spread(j, o, rel):
        first, second = rel if o else rel[::-1]
        flight["g", j, o, rel, 0].wait_recv()
        if second == 2 or (second == 0 and first == 2):
            flight["g", j, o, rel, 1].wait_recv()
        src = gath.at[j, o, SLOT[rel], core]
        ways = {3: 1, 1: -1}
        if second == 0:
            if first != 2:
                pass_on(j, o, rel, 1 - o, ways[first], halves[ways[first]], src)
            for way in (1, -1):
                pass_on(j, o, rel, o, way, whole, src)
        elif second != 2:
            pass_on(j, o, rel, o, ways[second], halves[ways[second]], src)
        cross(j, o, rel, src)

    def convert(j, s):
        for o in (0, 1):
            for i, rel in enumerate(SLOTS[4 * s : 4 * s + 4]):
                flight["gc", j, o, rel].wait_recv()
                for k in (0, 1):
                    spot = 2 * (2 * (i % 2) + k) + (j if i < 2 else 1 - j)
                    rows = gath[j, o, 4 * s + i, k]
                    top = rows.astype(BF16)
                    at = slice(16 * spot, 16 * (spot + 1))
                    rhs_hi[j, s, o, at, :] = top
                    rhs_lo[j, s, o, at, :] = (rows - top.astype(F32)).astype(BF16)

    def multiply(n, j, s):
        dims = (((1,), (1,)), ((), ()))
        total = None
        for o in (0, 1):
            for a, b in ((lhs_hi, rhs_hi), (lhs_hi, rhs_lo), (lhs_lo, rhs_hi)):
                term = lax.dot_general(a[n, o], b[j, s, o], dims, preferred_element_type=F32)
                total = term if total is None else total + term
        sent[n, j, s] = total.reshape(4, 64, 128)
        for i, to in enumerate((mate, near, far)):
            send(
                ("out", n, j, s, i),
                sent.at[n, j, s, 1 + i],
                got.at[n, j, s, i],
                out_s.at[n, j, s, i],
                out_r.at[n, j, s, i],
                to,
            )

    lane = lax.broadcasted_iota(jnp.int32, (64, 128), 1)
    left, first_half = lane < 64, lax.rem(lane // 16, 2) == 0

    def finish(n, s):
        parts = []
        for j in (0, 1):
            for i in range(3):
                flight["out", n, j, s, i].wait_recv()
            same = sent[n, j, s, 0] + got[n, j, s, 2]
            other = got[n, j, s, 0] + got[n, j, s, 1]
            parts.append((jnp.where(par == 0, same, other), jnp.where(par == 0, other, same)))
        for i in (0, 1):
            merged = []
            for low, high in zip(*parts):
                if i:
                    low, high = pltpu.roll(low, 112, 1), pltpu.roll(high, 16, 1)
                merged.append(jnp.where(first_half, low, high))
            even, odd = merged
            fulls = (
                jnp.where(left, even, pltpu.roll(odd, 64, 1)),
                jnp.where(left, pltpu.roll(even, 64, 1), odd),
            )
            for full, rel in zip(fulls, SLOTS[4 * s + 2 * i : 4 * s + 2 * i + 2]):
                block = lax.rem(y + rel[0], 4) * 4 + lax.rem(x + rel[1], 4)
                cols = pl.ds(pl.multiple_of(block * 128, 128), 128)
                out_ref[:, 16 * n : 16 * (n + 1), cols] = full.reshape(4, 16, 128)

    steps = dict(
        project=project, add=add, pass1=pass1, close1=close1, close2=close2, close3=close3, lookup=lookup, weigh=weigh, scale=scale,
        begin=begin, spread=spread, convert=convert, multiply=multiply, finish=finish,
    )
    for name, *args in ORDER:
        steps[name](*args)
    for copy in started:
        copy.wait_send()


def per_device(pair_density, basis, block_slot, energy_code, freq_order):
    tr_dev = pair_density.shape[1]
    vmem, dma = pltpu.VMEM, pltpu.SemaphoreType.DMA
    any_space = pl.BlockSpec(memory_space=pl.ANY)
    in_vmem = pl.BlockSpec(memory_space=pltpu.VMEM)
    scratch = [
        vmem((640, 1024), BF16),
        vmem((640, 2048), BF16),
        vmem((2, 1024, 640), BF16),
        vmem((4, 2, 4, 4, 2, 2, 16, 256), F32),
        vmem((4, 2, 4, 4, 2, 16, 256), F32),
        vmem((4, 2, 6, 4, 16, 256), F32),
        vmem((4, 2, 4, 2, 16, 256), F32),
        vmem((4, 2, 3, 2, 16, 256), F32),
        vmem((4, 2, 2, 16, 256), F32),
        vmem((4, 2, 2, 16, 256), F32),
        vmem((2, 2, 2, 16, 1024), F32),
        vmem((2, 8, 1024), F32),
        vmem((2, 16, 8, 1024), F32),
        vmem((2, 2, 16, 2, 16, 1024), F32),
        vmem((2, 2, 256, 1024), BF16),
        vmem((2, 2, 256, 1024), BF16),
        vmem((2, 4, 2, 128, 1024), BF16),
        vmem((2, 4, 2, 128, 1024), BF16),
        vmem((2, 2, 4, 4, 64, 128), F32),
        vmem((2, 2, 4, 3, 64, 128), F32),
        dma((2,)),
        dma((4,)), dma((4,)),
        dma((4, 2, 6)), dma((4, 2, 6)),
        dma((4, 2, 3)), dma((4, 2, 3)),
        dma((4,)), dma((4,)),
        dma((4,)), dma((4,)),
        dma, dma,
        dma((2, 2, 16, 2)), dma((2, 2, 16, 2)),
        dma((2, 2, 16)), dma((2, 2, 16)),
        dma((2, 2, 4, 3)), dma((2, 2, 4, 3)),
    ]
    return pl.pallas_call(
        functools.partial(kernel, float(tr_dev * lax.axis_size("tr"))),
        out_shape=jax.ShapeDtypeStruct((4, 32, 2048), F32),
        in_specs=[pl.BlockSpec(memory_space=pltpu.SMEM), in_vmem, in_vmem, any_space, any_space],
        out_specs=in_vmem,
        scratch_shapes=scratch,
        compiler_params=pltpu.CompilerParams(
            collective_id=0, has_side_effects=True, vmem_limit_bytes=60 * 2**20
        ),
        name="polarizability",
    )(
        freq_order,
        block_slot.reshape(1, tr_dev),
        energy_code.reshape(1, tr_dev),
        pair_density,
        basis,
    )


def solution(mesh):
    placed = (P("pw", "tr"), P("pw", None), P("tr"), P("tr"), P())
    return jax.shard_map(
        per_device, mesh=mesh, in_specs=placed, out_specs=P("tr", "pw", None), check_vma=False
    )
```

```python
import functools

import jax
import jax.numpy as jnp
from jax import lax
from jax.experimental import pallas as pl
from jax.experimental.pallas import tpu as pltpu
from jax.sharding import PartitionSpec as P

F32 = jnp.float32
BF16 = jnp.bfloat16
MESH = pl.DeviceIdType.MESH

SLOTS = [
    (0, 0), (0, 1), (0, 3), (1, 0),
    (3, 0), (1, 1), (1, 3), (3, 1),
    (3, 3), (0, 2), (2, 0), (1, 2),
    (3, 2), (2, 1), (2, 3), (2, 2),
]
SLOT = {rel: i for i, rel in enumerate(SLOTS)}

ORDER = [
    ("project", 0), ("project", 1), ("project", 2), ("add", 0), ("project", 3), ("lookup",), ("weigh", 0),
    ("pass1", 0), ("add", 1), ("weigh", 1), ("close1", 0), ("pass1", 1), ("add", 2), ("close2", 0),
    ("close1", 1), ("pass1", 2), ("add", 3), ("close2", 1), ("close1", 2), ("pass1", 3), ("close3", 0),
    ("close2", 2), ("close1", 3), ("close3", 1), ("scale", 0, 0), ("begin", 0, 0), ("close2", 3),
    ("spread", 0, 0, (0, 3)), ("spread", 0, 0, (3, 0)), ("begin", 0, 1), ("scale", 0, 1),
    ("spread", 0, 0, (0, 1)), ("spread", 0, 0, (1, 0)), ("close3", 2), ("spread", 0, 0, (3, 3)),
    ("spread", 0, 0, (1, 3)), ("spread", 0, 1, (0, 1)), ("spread", 0, 1, (0, 3)), ("spread", 0, 0, (0, 2)),
    ("spread", 0, 1, (1, 0)), ("spread", 0, 1, (3, 0)), ("close3", 3), ("begin", 1, 0), ("convert", 0, 0),
    ("scale", 1, 0), ("spread", 0, 0, (2, 0)), ("spread", 0, 0, (3, 1)), ("spread", 0, 0, (1, 1)),
    ("multiply", 0, 0, 0), ("spread", 0, 1, (0, 2)), ("spread", 0, 0, (2, 3)), ("spread", 0, 1, (1, 3)),
    ("spread", 0, 0, (1, 2)), ("spread", 0, 1, (1, 1)), ("spread", 0, 0, (3, 2)), ("spread", 0, 1, (2, 0)),
    ("begin", 1, 1), ("spread", 0, 1, (3, 3)), ("spread", 0, 1, (3, 1)), ("scale", 1, 1),
    ("multiply", 1, 0, 0), ("convert", 0, 1), ("multiply", 1, 0, 1), ("spread", 0, 0, (2, 1)),
    ("spread", 0, 1, (1, 2)), ("spread", 1, 0, (1, 0)), ("spread", 1, 0, (0, 3)), ("spread", 1, 0, (3, 0)),
    ("spread", 1, 0, (0, 1)), ("spread", 0, 0, (2, 2)), ("multiply", 0, 0, 1), ("spread", 0, 1, (2, 1)),
    ("spread", 0, 1, (2, 3)), ("spread", 1, 1, (1, 0)), ("convert", 0, 2), ("multiply", 1, 0, 2),
    ("spread", 0, 1, (3, 2)), ("spread", 1, 1, (0, 3)), ("spread", 1, 1, (0, 1)), ("spread", 1, 1, (3, 0)),
    ("multiply", 0, 0, 2), ("spread", 1, 0, (0, 2)), ("spread", 1, 0, (3, 3)), ("convert", 1, 0),
    ("spread", 1, 0, (1, 3)), ("multiply", 1, 1, 0), ("spread", 0, 1, (2, 2)), ("spread", 1, 0, (2, 0)),
    ("spread", 1, 0, (1, 1)), ("spread", 1, 1, (1, 1)), ("spread", 1, 1, (1, 3)), ("spread", 1, 0, (3, 1)),
    ("multiply", 0, 1, 0), ("spread", 1, 1, (2, 0)), ("spread", 1, 1, (0, 2)), ("convert", 0, 3),
    ("multiply", 1, 0, 3), ("spread", 1, 0, (3, 2)), ("spread", 1, 1, (3, 3)), ("spread", 1, 1, (3, 1)),
    ("spread", 1, 0, (1, 2)), ("spread", 1, 0, (2, 3)), ("multiply", 0, 0, 3), ("spread", 1, 1, (1, 2)),
    ("spread", 1, 0, (2, 1)), ("convert", 1, 1), ("multiply", 1, 1, 1), ("spread", 1, 1, (2, 3)),
    ("spread", 1, 1, (2, 1)), ("multiply", 0, 1, 1), ("spread", 1, 1, (3, 2)), ("spread", 1, 0, (2, 2)),
    ("convert", 1, 2), ("multiply", 1, 1, 2), ("multiply", 0, 1, 2), ("spread", 1, 1, (2, 2)),
    ("finish", 0, 0), ("finish", 1, 0), ("convert", 1, 3), ("multiply", 1, 1, 3), ("multiply", 0, 1, 3),
    ("finish", 1, 1), ("finish", 0, 1), ("finish", 1, 2), ("finish", 0, 2), ("finish", 1, 3),
    ("finish", 0, 3),
]


def device(y, x, z, core):
    y, x, z = lax.rem(y + 4, 4), lax.rem(x + 4, 4), lax.rem(z + 8, 8)
    return ((y * 4 + x) * 2 + z // 4) * 2 + core, lax.rem(z, 4)


def kernel(
    trans,
    freq_ref, slot_ref, code_ref, pair_hbm, basis_hbm, out_ref,
    pair, basis, basis_t, part, mine, ring1, ring1_sum, ring2, ring2_sum, zrecv,
    proj, energy, weight, gath, lhs_hi, lhs_lo, rhs_hi, rhs_lo, sent, got,
    load_sem, core_s, core_r, ring1_s, ring1_r, ring2_s, ring2_r, z_s, z_r,
    mate_s, mate_r, en_s, en_r, gath_s, gath_r, gcore_s, gcore_r, out_s, out_r,
):
    pw, tr = lax.axis_index("pw"), lax.axis_index("tr")
    core, zh = lax.rem(pw, 2), lax.rem(pw // 2, 2)
    x, y = lax.rem(pw // 4, 4), pw // 16
    z = zh * 4 + tr
    par = lax.rem(z, 2)
    away = 1 - 2 * par

    partner = device(y, x, z, 1 - core)
    ydev = {d: device(y + d, x, z, core) for d in (1, -1, 2)}
    xdev = {d: device(y, x + d, z, core) for d in (1, -1, 2)}
    opposite = device(y, x, z + 4, core)
    z_mate, z_near, z_far = z + away, z - away, z + 2 * away
    mate, near = device(y, x, z_mate, core), device(y, x, z_near, core)
    far, far_from = device(y, x, z_far, core), device(y, x, z - 2 * away, core)

    load_pair = pltpu.make_async_copy(pair_hbm, pair, load_sem.at[0])
    load_basis = pltpu.make_async_copy(basis_hbm, basis, load_sem.at[1])
    load_basis.start()
    load_pair.start()

    barrier = pltpu.get_barrier_semaphore()
    peers = (partner, *ydev.values(), *xdev.values(), opposite, mate, near, far, far_from)
    for peer in peers:
        pl.semaphore_signal(barrier, inc=1, device_id=peer, device_id_type=MESH)

    flight = {}

    def send(key, src, dst, ssem, rsem, to):
        copy = pltpu.make_async_remote_copy(
            src_ref=src, dst_ref=dst, send_sem=ssem, recv_sem=rsem, device_id=to, device_id_type=MESH
        )
        copy.start()
        flight[key] = copy

    load_basis.wait()
    turned = basis[...].T.reshape(64, 2, 16, 640)
    for j in (0, 1):
        basis_t[j] = turned[:, j].reshape(1024, 640)
    load_pair.wait()

    place = ((y, x), (x, y))
    line = ((ydev, xdev), (xdev, ydev))

    def project(c):
        j, u = divmod(c, 2)
        cols = pair[:, 512 * u : 512 * (u + 1)]

        @pl.loop(0, 4)
        def _(i):
            rows = basis_t[j, pl.ds(pl.multiple_of(i * 256, 256), 256), :]
            block = jnp.dot(rows, cols, preferred_element_type=F32)
            for k in range(4):
                piece = block[64 * k : 64 * (k + 1)]
                part[c, 0, i, k] = piece[:, :256].reshape(2, 2, 16, 256)
                part[c, 1, k, i] = piece[:, 256:].reshape(2, 2, 16, 256)

        if c == 0:
            pl.semaphore_wait(barrier, len(peers))
        send(
            ("core", c), part.at[c, :, :, :, :, 1 - core], mine.at[c], core_s.at[c], core_r.at[c], partner
        )

    def add(c):
        flight["core", c].wait_recv()

        @pl.loop(0, 4)
        def _(i):
            mine[c, :, i] = mine[c, :, i] + part[c, :, i, :, :, core]

        for order in (0, 1):
            at, to = place[order][0], line[order][0]
            ahead, behind, across = (lax.rem(at + d, 4) for d in (1, 3, 2))
            pieces = ((across, 0, 1), (across, 1, -1), (ahead, 1, 1), (behind, 0, -1))
            for i, (p, half, way) in enumerate(pieces):
                send(
                    ("r1", c, order, i),
                    mine.at[c, order, p, :, half],
                    ring1.at[c, order, i],
                    ring1_s.at[c, order, i],
                    ring1_r.at[c, order, i],
                    to[way],
                )

    def pass1(c):
        for order in (0, 1):
            at, to = place[order][0], line[order][0]
            for i, (p, way) in enumerate(((lax.rem(at + 1, 4), 1), (lax.rem(at + 3, 4), -1))):
                flight["r1", c, order, i].wait_recv()
                ring1[c, order, i] = ring1[c, order, i] + mine[c, order, p, :, i]
                send(
                    ("r1", c, order, 4 + i),
                    ring1.at[c, order, i],
                    ring1.at[c, order, 4 + i],
                    ring1_s.at[c, order, 4 + i],
                    ring1_r.at[c, order, 4 + i],
                    to[way],
                )

    def close1(c):
        for order in (0, 1):
            at = place[order][0]
            for i in (2, 3, 4, 5):
                flight["r1", c, order, i].wait_recv()
            for half, i, k in ((0, 3, 4), (1, 2, 5)):
                ring1_sum[c, order, :, half] = mine[c, order, at, :, half] + ring1[c, order, i] + ring1[c, order, k]
            at, to = place[order][1], line[order][1]
            for i, way in enumerate((2, 1, -1)):
                send(
                    ("r2", c, order, i),
                    ring1_sum.at[c, order, lax.rem(at + way + 4, 4)],
                    ring2.at[c, order, i],
                    ring2_s.at[c, order, i],
                    ring2_r.at[c, order, i],
                    to[way],
                )

    def close2(c):
        for order in (0, 1):
            at = place[order][1]
            for i in range(3):
                flight["r2", c, order, i].wait_recv()
            ring2_sum[c, order] = (ring1_sum[c, order, at] + ring2[c, order, 0]) + (
                ring2[c, order, 1] + ring2[c, order, 2]
            )
        send(("z", c), ring2_sum.at[c], zrecv.at[c], z_s.at[c], z_r.at[c], opposite)

    def close3(c):
        j, u = divmod(c, 2)
        flight["z", c].wait_recv()
        for order in (0, 1):
            first = 512 * u + 256 * order
            proj[0, j, :, :, first : first + 256] = ring2_sum[c, order] + zrecv[c, order]
        cols = pl.ds(512 * u, 512)
        send(
            ("mate", c),
            proj.at[0, j, :, :, cols],
            proj.at[1, j, :, :, cols],
            mate_s.at[c],
            mate_r.at[c],
            mate,
        )

    def lookup():
        slots = slot_ref[...] - tr * slot_ref.shape[1]
        codes = jnp.broadcast_to(code_ref[...], (16, code_ref.shape[1]))
        high = (codes >> 7).astype(F32).astype(BF16)
        low = (codes & 127).astype(F32).astype(BF16)
        total = jnp.zeros((16, 1024), F32)
        for i in range(4):
            js = lax.broadcasted_iota(jnp.int32, (256, 1024), 0) + 256 * i
            hot = jnp.where(js == slots, 1.0, 0.0).astype(BF16)
            total = total + 128.0 * jnp.dot(high[:, 256 * i : 256 * (i + 1)], hot, preferred_element_type=F32)
            total = total + jnp.dot(low[:, 256 * i : 256 * (i + 1)], hot, preferred_element_type=F32)
        energy[0] = total[:8] / 1024.0
        send("energy", energy.at[0], energy.at[1], en_s, en_r, mate)

    def weigh(o):
        if o == 1:
            flight["energy"].wait_recv()
        e = energy[o]
        for k in range(16):
            order = jnp.full((8, 1024), freq_ref[k].astype(F32), F32)
            f = jnp.exp2(order * 0.5 - 4.0)
            weight[o, k] = 2.0 * e / (e * e + f * f) / trans

    def scale(j, o):
        for i, target in enumerate((z, z_mate, z_near, z_far)):
            target = lax.rem(target + 8, 8)
            rows = proj[o, j, target // 4].reshape(2, 8, 1024)
            for k in range(4):
                w = weight[o, lax.rem(target, 4) * 4 + k]
                scaled = (rows * w[None]).reshape(16, 1024)
                top = scaled.astype(BF16)
                at = slice(64 * i + 16 * k, 64 * i + 16 * (k + 1))
                lhs_hi[j, o, at, :] = top
                lhs_lo[j, o, at, :] = (scaled - top.astype(F32)).astype(BF16)

    whole, halves = (0, 16), {1: (0, 8), -1: (8, 8)}

    def pass_on(j, o, rel, axis, way, rows, src):
        dy, dx = rel
        there = (dy, (dx - way) % 4) if axis else ((dy - way) % 4, dx)
        slot, half, rows = SLOT[there], int(rows[0] > 0), pl.ds(*rows)
        send(
            ("g", j, o, there, half),
            src.at[rows],
            gath.at[j, o, slot, core, rows],
            gath_s.at[j, o, slot, half],
            gath_r.at[j, o, slot, half],
            (xdev if axis else ydev)[way],
        )

    def cross(j, o, rel, src):
        slot = SLOT[rel]
        send(
            ("gc", j, o, rel), src, gath.at[j, o, slot, core], gcore_s.at[j, o, slot], gcore_r.at[j, o, slot], partner
        )

    def begin(j, o):
        if o == 1:
            for u in (0, 1):
                flight["mate", 2 * j + u].wait_recv()
        own = proj.at[o, j, par]
        for axis in (1 - o, o):
            for way in (1, -1):
                pass_on(j, o, (0, 0), axis, way, whole, own)
        cross(j, o, (0, 0), own)
        gath[j, o, 0, core] = own[...]

    def spread(j, o, rel):
        first, second = rel if o else rel[::-1]
        flight["g", j, o, rel, 0].wait_recv()
        if second == 2 or (second == 0 and first == 2):
            flight["g", j, o, rel, 1].wait_recv()
        src = gath.at[j, o, SLOT[rel], core]
        ways = {3: 1, 1: -1}
        if second == 0:
            if first != 2:
                pass_on(j, o, rel, 1 - o, ways[first], halves[ways[first]], src)
            for way in (1, -1):
                pass_on(j, o, rel, o, way, whole, src)
        elif second != 2:
            pass_on(j, o, rel, o, ways[second], halves[ways[second]], src)
        cross(j, o, rel, src)

    def convert(j, s):
        for o in (0, 1):
            for i, rel in enumerate(SLOTS[4 * s : 4 * s + 4]):
                flight["gc", j, o, rel].wait_recv()
                for k in (0, 1):
                    spot = 2 * (2 * (i % 2) + k) + (j if i < 2 else 1 - j)
                    rows = gath[j, o, 4 * s + i, k]
                    top = rows.astype(BF16)
                    at = slice(16 * spot, 16 * (spot + 1))
                    rhs_hi[j, s, o, at, :] = top
                    rhs_lo[j, s, o, at, :] = (rows - top.astype(F32)).astype(BF16)

    def multiply(n, j, s):
        dims = (((1,), (1,)), ((), ()))
        total = None
        for o in (0, 1):
            for a, b in ((lhs_hi, rhs_hi), (lhs_hi, rhs_lo), (lhs_lo, rhs_hi)):
                term = lax.dot_general(a[n, o], b[j, s, o], dims, preferred_element_type=F32)
                total = term if total is None else total + term
        sent[n, j, s] = total.reshape(4, 64, 128)
        for i, to in ((2, far), (1, near), (0, mate)):
            send(
                ("out", n, j, s, i),
                sent.at[n, j, s, 1 + i],
                got.at[n, j, s, i],
                out_s.at[n, j, s, i],
                out_r.at[n, j, s, i],
                to,
            )

    lane = lax.broadcasted_iota(jnp.int32, (64, 128), 1)
    left, first_half = lane < 64, lax.rem(lane // 16, 2) == 0

    def finish(n, s):
        parts = []
        for j in (0, 1):
            for i in range(3):
                flight["out", n, j, s, i].wait_recv()
            same = sent[n, j, s, 0] + got[n, j, s, 2]
            other = got[n, j, s, 0] + got[n, j, s, 1]
            parts.append((jnp.where(par == 0, same, other), jnp.where(par == 0, other, same)))
        for i in (0, 1):
            merged = []
            for low, high in zip(*parts):
                if i:
                    low, high = pltpu.roll(low, 112, 1), pltpu.roll(high, 16, 1)
                merged.append(jnp.where(first_half, low, high))
            even, odd = merged
            fulls = (
                jnp.where(left, even, pltpu.roll(odd, 64, 1)),
                jnp.where(left, pltpu.roll(even, 64, 1), odd),
            )
            for full, rel in zip(fulls, SLOTS[4 * s + 2 * i : 4 * s + 2 * i + 2]):
                block = lax.rem(y + rel[0], 4) * 4 + lax.rem(x + rel[1], 4)
                cols = pl.ds(pl.multiple_of(block * 128, 128), 128)
                out_ref[:, 16 * n : 16 * (n + 1), cols] = full.reshape(4, 16, 128)
        for j in (0, 1):
            for i in range(3):
                flight["out", n, j, s, i].wait_send()

    steps = dict(
        project=project, add=add, pass1=pass1, close1=close1, close2=close2, close3=close3, lookup=lookup, weigh=weigh, scale=scale,
        begin=begin, spread=spread, convert=convert, multiply=multiply, finish=finish,
    )
    last = max(i for i, step in enumerate(ORDER) if step[0] == "multiply")
    for i, (name, *args) in enumerate(ORDER):
        steps[name](*args)
        if i == last:
            for key, copy in flight.items():
                if key[0] != "out":
                    copy.wait_send()


def per_device(pair_density, basis, block_slot, energy_code, freq_order):
    tr_dev = pair_density.shape[1]
    vmem, dma = pltpu.VMEM, pltpu.SemaphoreType.DMA
    any_space = pl.BlockSpec(memory_space=pl.ANY)
    in_vmem = pl.BlockSpec(memory_space=pltpu.VMEM)
    scratch = [
        vmem((640, 1024), BF16),
        vmem((640, 2048), BF16),
        vmem((2, 1024, 640), BF16),
        vmem((4, 2, 4, 4, 2, 2, 16, 256), F32),
        vmem((4, 2, 4, 4, 2, 16, 256), F32),
        vmem((4, 2, 6, 4, 16, 256), F32),
        vmem((4, 2, 4, 2, 16, 256), F32),
        vmem((4, 2, 3, 2, 16, 256), F32),
        vmem((4, 2, 2, 16, 256), F32),
        vmem((4, 2, 2, 16, 256), F32),
        vmem((2, 2, 2, 16, 1024), F32),
        vmem((2, 8, 1024), F32),
        vmem((2, 16, 8, 1024), F32),
        vmem((2, 2, 16, 2, 16, 1024), F32),
        vmem((2, 2, 256, 1024), BF16),
        vmem((2, 2, 256, 1024), BF16),
        vmem((2, 4, 2, 128, 1024), BF16),
        vmem((2, 4, 2, 128, 1024), BF16),
        vmem((2, 2, 4, 4, 64, 128), F32),
        vmem((2, 2, 4, 3, 64, 128), F32),
        dma((2,)),
        dma((4,)), dma((4,)),
        dma((4, 2, 6)), dma((4, 2, 6)),
        dma((4, 2, 3)), dma((4, 2, 3)),
        dma((4,)), dma((4,)),
        dma((4,)), dma((4,)),
        dma, dma,
        dma((2, 2, 16, 2)), dma((2, 2, 16, 2)),
        dma((2, 2, 16)), dma((2, 2, 16)),
        dma((2, 2, 4, 3)), dma((2, 2, 4, 3)),
    ]
    return pl.pallas_call(
        functools.partial(kernel, float(tr_dev * lax.axis_size("tr"))),
        out_shape=jax.ShapeDtypeStruct((4, 32, 2048), F32),
        in_specs=[pl.BlockSpec(memory_space=pltpu.SMEM), in_vmem, in_vmem, any_space, any_space],
        out_specs=in_vmem,
        scratch_shapes=scratch,
        compiler_params=pltpu.CompilerParams(
            collective_id=0, has_side_effects=True, vmem_limit_bytes=60 * 2**20
        ),
        name="polarizability",
    )(
        freq_order,
        block_slot.reshape(1, tr_dev),
        energy_code.reshape(1, tr_dev),
        pair_density,
        basis,
    )


def solution(mesh):
    placed = (P("pw", "tr"), P("pw", None), P("tr"), P("tr"), P())
    return jax.shard_map(
        per_device, mesh=mesh, in_specs=placed, out_specs=P("tr", "pw", None), check_vma=False
    )
```
